32 devices in a mesh: seg: 8 (over z, core), chan: 4 (over y, x).
Axes of the slice: x: 2, y: 2, z: 4, core: 2. Of those that a mesh axis runs over, the one named last changes fastest.
Arguments:
- signal: bfloat16 [4096, 16384], P('chan', 'seg'), may hold values from -64 to 64
- spatial: float32 [4096, 64], P('chan'), may hold values from -0.09375 to 0.09375
- temporal: float32 [64, 256], replicated, may hold values from -5 to 5
- start_codes: float32 [64, 16384], P(None, 'seg'), may hold values from -1.2 to 1.2
- thresholds: float32 [64], replicated, may hold values from 0.05 to 0.3
- step_sizes: float32 [64], replicated, may hold values from 0.03 to 0.1
- breaks: int32 [16], replicated, may hold values from 0 to 16383, as said below
Outputs:
- final_codes: float32 [64, 16384], P(None, 'seg')
- space_atoms: float32 [4096, 64], P('chan')
- time_atoms: float32 [64, 256], replicated
The draws below stay inside these ranges and needn't reach their ends.
Inputs may be any that keep to these rules, and one draw needn't show every extreme that they name: `breaks`: Increasing; one break lies in each of the 16 equal stretches of the window.
All inputs are finite; a program needn't handle non-finite values.
Results may differ from the reference program's by a relative error of at most 0.0058.
Values may be sent and summed in bfloat16 or wider, within the bound.
A program may use at most 128 MiB of HBM per device.

```python
import math
import jax
import jax.numpy as jnp
from jax import lax

C = 4096
K = 64
L = 256
ITERS = 10
OUTER = 2
NB = 16
TIME = 16384


def draw_signal(key, part):
    chan_key, time_key, noise_key = jax.random.split(key, 3)
    rising = jnp.exp(jnp.log(3.0) * jnp.arange(C, dtype=jnp.float32) / C)
    chan_scale = rising * jnp.exp(jax.random.uniform(chan_key, (C,), jnp.float32, -0.6931, 0.6931))
    time_scale = jnp.exp(jax.random.uniform(time_key, (TIME,), jnp.float32, -0.6931, 0.6931))
    noise_field = jnp.clip(jax.random.normal(noise_key, (C, TIME), jnp.float32), -4.0, 4.0)
    return (chan_scale[:, None] * time_scale[None, :] * noise_field).astype(jnp.bfloat16)


def draw_breaks(key, part):
    stretch = TIME // NB
    offsets = jax.random.randint(key, (NB,), 0, stretch, dtype=jnp.int32)
    return (jnp.arange(NB, dtype=jnp.int32) * stretch + offsets).astype(jnp.int32)


def level_of(own_key, dims, cuts, smallest, largest):
    level, own = 1.0, jax.random.fold_in(own_key, 6)
    for dim, parts in cuts:
        steps = jnp.exp(jax.random.uniform(jax.random.fold_in(own, dim), (parts,), jnp.float32, smallest / len(cuts), largest / len(cuts)))
        level = level * jnp.repeat(steps, dims[dim] // parts).reshape([-1 if axis == dim else 1 for axis in range(len(dims))])
    return level


def normal_values(stream_key, shape, width, reach, shards=(), held_as=jnp.bfloat16):
    drawn = jax.random.normal(stream_key, shape, jnp.float32) * width
    if len(shards) > 0:
        drawn = level_of(stream_key, shape, shards, -0.22, 0.18) * drawn
    return jnp.clip(drawn, min=-reach, max=reach).astype(held_as)


def setup_inputs(seed: int = 0) -> dict:
    streams_of = jax.random.split(jax.random.key(seed), 8)
    signal = draw_signal(jax.random.fold_in(streams_of[7], 71), 0)
    spatial = normal_values(streams_of[1], (C, K), C ** -0.5, 0.09375, ((0, 4),), jnp.float32)
    temporal = normal_values(streams_of[2], (K, L), 1.0, 5.0, (), jnp.float32)
    start_codes = normal_values(streams_of[3], (K, TIME), 0.3, 1.2, ((1, 8),), jnp.float32)
    thresholds = jnp.clip(jnp.exp(jax.random.uniform(streams_of[4], (K,), jnp.float32, math.log(0.05), math.log(0.3))), 0.05, 0.3)
    step_sizes = jnp.clip(jnp.exp(jax.random.uniform(streams_of[5], (K,), jnp.float32, math.log(0.03), math.log(0.1))), 0.03, 0.1)
    breaks = draw_breaks(jax.random.fold_in(streams_of[7], 71), 0)
    return dict(signal=signal, spatial=spatial, temporal=temporal, start_codes=start_codes, thresholds=thresholds, step_sizes=step_sizes, breaks=breaks)


epsilon = 1e-06
highest = lax.Precision.HIGHEST

def rounded(values):
    return lax.optimization_barrier(values.astype(jnp.bfloat16)).astype(jnp.float32)

def unit_columns(matrix):
    return matrix / jnp.sqrt(lax.optimization_barrier(jnp.sum(matrix * matrix, axis=0, keepdims=True)) + epsilon)

def unit_rows(matrix):
    return matrix / jnp.sqrt(lax.optimization_barrier(jnp.sum(matrix * matrix, axis=1, keepdims=True)) + epsilon)

def spectrum(values):
    return jnp.fft.rfft(values, n=2 * TIME, axis=-1)

def convolve(kernel, latent):
    return jnp.fft.irfft(spectrum(kernel) * spectrum(latent), n=2 * TIME, axis=-1)[:, :TIME]

def correlate(kernel, residual):
    return jnp.fft.irfft(jnp.conj(spectrum(kernel)) * spectrum(residual), n=2 * TIME, axis=-1)[:, :TIME]

def lag_stats(residual, latent):
    return jnp.fft.irfft(spectrum(residual) * jnp.conj(spectrum(latent)), n=2 * TIME, axis=-1)[:, :L]

def reference(signal, spatial, temporal, start_codes, thresholds, step_sizes, breaks):
    positions = jnp.arange(TIME, dtype=jnp.int32)
    crosses = (positions[None, :] < breaks[:, None]) & (breaks[:, None] < positions[None, :] + L)
    allowed = jnp.where(jnp.any(crosses, axis=0), 0.0, 1.0).astype(jnp.float32)
    space_atoms = unit_columns(spatial)
    kernel = unit_rows(temporal)
    gram_matrix = jnp.dot(space_atoms.T, space_atoms, precision=highest)
    latent = start_codes
    step_col = step_sizes[:, None]
    limit_col = (step_sizes * thresholds)[:, None]
    for sweep_index in range(OUTER):
        projected = jnp.dot(space_atoms.astype(jnp.bfloat16).T, signal, preferred_element_type=jnp.float32)
        kernel_r = rounded(kernel)
        for iteration in range(ITERS):
            rebuilt = convolve(kernel_r, rounded(latent))
            residual = projected - jnp.dot(gram_matrix, rebuilt, precision=highest)
            descent = correlate(kernel_r, rounded(residual))
            stepped = latent + step_col * descent
            latent = allowed[None, :] * jnp.sign(stepped) * jnp.maximum(jnp.abs(stepped) - limit_col, 0.0)
        latent_r = rounded(latent)
        rebuilt = convolve(kernel_r, latent_r)
        row_stats = jnp.dot(signal, rebuilt.astype(jnp.bfloat16).T, preferred_element_type=jnp.float32)
        cross_gram = jnp.dot(rebuilt, rebuilt.T, precision=highest)
        raw_space = row_stats - jnp.dot(space_atoms, cross_gram - jnp.diag(jnp.diag(cross_gram)), precision=highest)
        others = projected - jnp.dot(gram_matrix - jnp.diag(jnp.diag(gram_matrix)), rebuilt, precision=highest)
        raw_kernel = lag_stats(others, latent_r)
        space_atoms = unit_columns(raw_space)
        kernel = unit_rows(raw_kernel)
        gram_matrix = jnp.dot(space_atoms.T, space_atoms, precision=highest)
    return (latent, space_atoms, kernel)
```

```python
import functools
import jax
import jax.numpy as jnp
from jax import lax
from jax.experimental import pallas as pl
from jax.experimental.pallas import tpu as pltpu
from jax.sharding import PartitionSpec as P

ITERS = 10
OUTER = 2
LANES = 128
HALO = 12


epsilon = 1e-06
highest = lax.Precision.HIGHEST


def passed_along(value, axis, steps):
    count = lax.axis_size(axis)
    leading, last = (max(0, -steps), min(count, count - steps))
    return lax.ppermute(value, axis, [(source, source + steps) for source in range(leading, last)])


def split3(matrix):
    high = matrix.astype(jnp.bfloat16)
    low = (matrix - high.astype(jnp.float32)).astype(jnp.bfloat16)
    return jnp.concatenate([high, high, low], axis=1)


def steps_kernel(
    steps, last, atoms, blocks, own,
    step_ref, limit_ref, latent_in, proj_in, taps_ref, flipped_ref, gram_ref, plain_ref,
    allowed_ref, inside_ref,
    *rest,
):
    if last:
        latent_out, rebuilt_out, lags_out, latent, proj, mixed, forward, backward = rest
    else:
        latent_out, latent, proj, mixed, forward, backward = rest

    def spread(block, carry):
        rows = pl.ds(pl.multiple_of(block * atoms, atoms), atoms)
        columns = pl.ds(pl.multiple_of(block * LANES, LANES), LANES)
        latent[rows, :] = latent_in[:, columns]
        proj[rows, :] = proj_in[:, columns]
        return carry

    lax.fori_loop(0, blocks, spread, 0)

    def build(atom, carry):
        for source, target in ((taps_ref, forward), (flipped_ref, backward)):
            row = jnp.broadcast_to(source[pl.ds(atom, 1), :], (LANES, 4 * LANES))
            turned = pltpu.roll(row, 0, 1, stride=1, stride_axis=0).astype(jnp.bfloat16)
            for part in range(3):
                target[atom, part * LANES : (part + 1) * LANES, :] = turned[
                    :, part * LANES : (part + 1) * LANES
                ]
        return carry

    lax.fori_loop(0, atoms, build, 0)

    def rows_of(atom):
        return pl.ds(atom, blocks, stride=atoms)

    def window(values):
        return jnp.concatenate(
            [values, pltpu.roll(values, 1, 0), pltpu.roll(values, 2, 0)], axis=1
        ).astype(jnp.bfloat16)

    def convolve(atom, carry):
        mixed[rows_of(atom), :] = jnp.dot(
            window(latent[rows_of(atom), :]), forward[atom], preferred_element_type=jnp.float32
        )
        return carry

    def mix(block, carry, matrix_ref):
        rows = pl.ds(pl.multiple_of(block * atoms, atoms), atoms)
        rebuilt = mixed[rows, :]
        high = rebuilt.astype(jnp.bfloat16)
        low = (rebuilt - high.astype(jnp.float32)).astype(jnp.bfloat16)
        stacked = jnp.concatenate([high, low, high], axis=0)
        mixed[rows, :] = proj[rows, :] - jnp.dot(
            matrix_ref[...], stacked, preferred_element_type=jnp.float32
        )
        return carry

    def shrink(atom, carry):
        residual = jnp.where(inside_ref[...] > 0.5, mixed[rows_of(atom), :], 0.0)
        ahead = pltpu.roll(residual, blocks - 1, 0)
        further = pltpu.roll(residual, blocks - 2, 0)
        descent = jnp.dot(
            jnp.concatenate([further, ahead, residual], axis=1).astype(jnp.bfloat16),
            backward[atom],
            preferred_element_type=jnp.float32,
        )
        limit = limit_ref[atom]
        stepped = latent[rows_of(atom), :] + step_ref[atom] * descent
        latent[rows_of(atom), :] = allowed_ref[...] * (
            stepped - jnp.minimum(jnp.maximum(stepped, -limit), limit)
        )
        return carry

    def one_step(iteration, carry):
        lax.fori_loop(0, atoms, convolve, 0, unroll=8)
        lax.fori_loop(0, blocks, functools.partial(mix, matrix_ref=gram_ref), 0, unroll=4)
        lax.fori_loop(0, atoms, shrink, 0, unroll=8)
        return carry

    lax.fori_loop(0, steps, one_step, 0)
    for block in range(own):
        first = (HALO + block) * atoms
        latent_out[:, block * LANES : (block + 1) * LANES] = latent[first : first + atoms, :]
    if not last:
        return
    lax.fori_loop(0, atoms, convolve, 0, unroll=8)
    for block in range(own):
        first = (HALO + block) * atoms
        rebuilt_out[:, block * LANES : (block + 1) * LANES] = mixed[first : first + atoms, :]
    lax.fori_loop(HALO, HALO + own, functools.partial(mix, matrix_ref=plain_ref), 0, unroll=4)

    def lagged(atom, carry):
        codes = latent[rows_of(atom), :]
        codes = jnp.concatenate([pltpu.roll(codes, 2, 0), pltpu.roll(codes, 1, 0), codes], axis=1)
        codes = codes[HALO - 4 : HALO + own + 4]
        others = mixed[rows_of(atom), :][HALO - 4 : HALO + own + 4]
        place = lax.broadcasted_iota(jnp.int32, others.shape, 0)
        others = jnp.where((place >= 4) & (place < own + 4), others, 0.0)
        high = others.astype(jnp.bfloat16).astype(jnp.float32)
        pair = jnp.concatenate([high, others - high], axis=0).astype(jnp.bfloat16)
        twice = jnp.concatenate([codes, codes], axis=0).astype(jnp.bfloat16)
        total = lax.dot_general(
            pair, twice, (((0,), (0,)), ((), ())), preferred_element_type=jnp.float32
        )
        half = LANES // 2
        while half >= 1:
            total = total[:half] + pltpu.roll(total[half:], 3 * LANES - half, 1)
            half //= 2
        lags_out[pl.ds(atom, 1), :] = total
        return carry

    lax.fori_loop(0, atoms, lagged, 0, unroll=2)


def run_steps(steps, last, latent, projected, kernel_b, gram_matrix, step, limit, allowed, inside):
    atoms, width = latent.shape
    blocks = width // LANES
    own = blocks - 2 * HALO
    taps = kernel_b.astype(jnp.float32)
    tap_count = taps.shape[1]
    forward = jnp.pad(taps, ((0, 0), (0, 4 * LANES - tap_count)))
    backward = jnp.pad(taps[:, ::-1], ((0, 0), (1, 4 * LANES - tap_count - 1)))
    plain = gram_matrix - jnp.diag(jnp.diag(gram_matrix))
    out = [jax.ShapeDtypeStruct((atoms, own * LANES), jnp.float32)]
    if last:
        out.append(jax.ShapeDtypeStruct((atoms, own * LANES), jnp.float32))
        out.append(jax.ShapeDtypeStruct((atoms, 3 * LANES), jnp.float32))
    in_vmem = pl.BlockSpec(memory_space=pltpu.VMEM)
    in_smem = pl.BlockSpec(memory_space=pltpu.SMEM)
    return pl.pallas_call(
        functools.partial(steps_kernel, steps, last, atoms, blocks, own),
        out_shape=out,
        in_specs=[in_smem] * 2 + [in_vmem] * 8,
        out_specs=[in_vmem] * len(out),
        scratch_shapes=[pltpu.VMEM((blocks * atoms, LANES), jnp.float32)] * 3
        + [pltpu.VMEM((atoms, 3 * LANES, LANES), jnp.bfloat16)] * 2,
        compiler_params=pltpu.CompilerParams(vmem_limit_bytes=48 * 1024 * 1024),
        cost_estimate=pl.CostEstimate(
            flops=4 * steps * atoms * width * 3 * LANES, bytes_accessed=8 * atoms * width, transcendentals=0
        ),
    )(
        step, limit, latent, projected, forward, backward, split3(gram_matrix), split3(plain),
        allowed.reshape(blocks, LANES), inside.reshape(blocks, LANES),
    )


def widened(value):
    rim = HALO * LANES
    before = passed_along(value[:, value.shape[1] - rim :], "seg", 1)
    after = passed_along(value[:, :rim], "seg", -1)
    return jnp.concatenate([before, value, after], axis=1)


def on_device(signal, spatial, temporal, start_codes, thresholds, step_sizes, breaks):
    chan_rows, seg_len = signal.shape
    atoms_all, tap_count = temporal.shape
    rim = HALO * LANES
    positions = lax.axis_index("seg") * seg_len - rim + lax.iota(jnp.int32, seg_len + 2 * rim)
    inside = (positions >= 0) & (positions < seg_len * lax.axis_size("seg"))
    crosses = (positions[None, :] < breaks[:, None]) & (
        breaks[:, None] < positions[None, :] + tap_count
    )
    allowed = jnp.where(jnp.any(crosses, axis=0) | ~inside, 0.0, 1.0).astype(jnp.float32)
    inside = inside.astype(jnp.float32)
    raw_start = lax.psum(jnp.dot(spatial.T, spatial, precision=highest), "chan")
    scaling = 1.0 / jnp.sqrt(jnp.diag(raw_start) + epsilon)
    space_loc = spatial * scaling[None, :]
    gram_matrix = raw_start * scaling[:, None] * scaling[None, :]
    kernel = temporal / jnp.sqrt(jnp.sum(temporal * temporal, axis=1, keepdims=True) + epsilon)
    latent = start_codes
    limits = step_sizes * thresholds
    rows_share = chan_rows // lax.axis_size("seg")
    for sweep_index in range(OUTER):
        space_b = space_loc.astype(jnp.bfloat16)
        kernel_b = kernel.astype(jnp.bfloat16)
        projected = lax.psum(jnp.dot(space_b.T, signal, preferred_element_type=jnp.float32), "chan")
        wide = widened(projected)
        (latent,) = run_steps(
            ITERS // 2, False, widened(latent), wide, kernel_b, gram_matrix,
            step_sizes, limits, allowed, inside,
        )
        latent, rebuilt, lags = run_steps(
            ITERS - ITERS // 2, True, widened(latent), wide, kernel_b, gram_matrix,
            step_sizes, limits, allowed, inside,
        )
        taps_part = lags[:, 1 : tap_count + 1][:, ::-1]
        rebuilt_b = rebuilt.astype(jnp.bfloat16)
        stats_rows = lax.psum_scatter(
            jnp.dot(signal, rebuilt_b.T, preferred_element_type=jnp.float32),
            "seg",
            scatter_dimension=0,
            tiled=True,
        )
        summed = lax.psum(
            jnp.concatenate(
                [jnp.dot(rebuilt, rebuilt.T, precision=highest), taps_part], axis=1
            ),
            "seg",
        )
        cross_gram, raw_kernel = summed[:, :atoms_all], summed[:, atoms_all:]
        seg_first = lax.axis_index("seg") * rows_share
        own_space = lax.dynamic_slice_in_dim(space_loc, seg_first, rows_share, 0)
        raw_rows = stats_rows - jnp.dot(
            own_space, cross_gram - jnp.diag(jnp.diag(cross_gram)), precision=highest
        )
        squares = lax.psum(jnp.sum(raw_rows * raw_rows, axis=0), ("seg", "chan"))
        new_rows = raw_rows / jnp.sqrt(squares + epsilon)[None, :]
        space_loc = lax.all_gather(new_rows, "seg", axis=0, tiled=True)
        if sweep_index + 1 < OUTER:
            gram_matrix = lax.psum(jnp.dot(space_loc.T, space_loc, precision=highest), "chan")
        kernel = raw_kernel / jnp.sqrt(
            jnp.sum(raw_kernel * raw_kernel, axis=1, keepdims=True) + epsilon
        )
    return (latent, space_loc, kernel)


def solution(mesh):
    placed = (P("chan", "seg"), P("chan", None), P(), P(None, "seg"), P(), P(), P())
    return jax.shard_map(
        on_device,
        mesh=mesh,
        in_specs=placed,
        out_specs=(P(None, "seg"), P("chan", None), P()),
        check_vma=False,
    )
```

```python
import functools
import jax
import jax.numpy as jnp
from jax import lax
from jax.experimental import pallas as pl
from jax.experimental.pallas import tpu as pltpu
from jax.sharding import PartitionSpec as P

ITERS = 10
OUTER = 2
LANES = 128
HALO = 12


epsilon = 1e-06
highest = lax.Precision.HIGHEST


def passed_along(value, axis, steps):
    count = lax.axis_size(axis)
    leading, last = (max(0, -steps), min(count, count - steps))
    return lax.ppermute(value, axis, [(source, source + steps) for source in range(leading, last)])


def split3(matrix):
    high = matrix.astype(jnp.bfloat16)
    low = (matrix - high.astype(jnp.float32)).astype(jnp.bfloat16)
    return jnp.concatenate([high, high, low], axis=1)


def steps_kernel(
    steps, last, atoms, blocks, own,
    step_ref, limit_ref, latent_in, proj_in, taps_ref, flipped_ref, gram_ref, plain_ref,
    allowed_ref, inside_ref,
    *rest,
):
    if last:
        latent_out, rebuilt_out, lags_out, latent, proj, mixed, forward, backward = rest
    else:
        latent_out, latent, proj, mixed, forward, backward = rest

    def spread(block, carry):
        rows = pl.ds(pl.multiple_of(block * atoms, atoms), atoms)
        columns = pl.ds(pl.multiple_of(block * LANES, LANES), LANES)
        latent[rows, :] = latent_in[:, columns]
        proj[rows, :] = proj_in[:, columns]
        return carry

    lax.fori_loop(0, blocks, spread, 0)

    def build(atom, carry):
        for source, target in ((taps_ref, forward), (flipped_ref, backward)):
            row = jnp.broadcast_to(source[pl.ds(atom, 1), :], (LANES, 4 * LANES))
            turned = pltpu.roll(row, 0, 1, stride=1, stride_axis=0).astype(jnp.bfloat16)
            for part in range(3):
                target[atom, part * LANES : (part + 1) * LANES, :] = turned[
                    :, part * LANES : (part + 1) * LANES
                ]
        return carry

    lax.fori_loop(0, atoms, build, 0)

    def rows_of(atom):
        return pl.ds(atom, blocks, stride=atoms)

    def window(values):
        return jnp.concatenate(
            [values, pltpu.roll(values, 1, 0), pltpu.roll(values, 2, 0)], axis=1
        ).astype(jnp.bfloat16)

    def convolve(atom, carry):
        mixed[rows_of(atom), :] = jnp.dot(
            window(latent[rows_of(atom), :]), forward[atom], preferred_element_type=jnp.float32
        )
        return carry

    def mix(block, carry, matrix_ref):
        rows = pl.ds(pl.multiple_of(block * atoms, atoms), atoms)
        rebuilt = mixed[rows, :]
        high = rebuilt.astype(jnp.bfloat16)
        low = (rebuilt - high.astype(jnp.float32)).astype(jnp.bfloat16)
        stacked = jnp.concatenate([high, low, high], axis=0)
        mixed[rows, :] = proj[rows, :] - jnp.dot(
            matrix_ref[...], stacked, preferred_element_type=jnp.float32
        )
        return carry

    def shrink(atom, carry):
        residual = jnp.where(inside_ref[...] > 0.5, mixed[rows_of(atom), :], 0.0)
        ahead = pltpu.roll(residual, blocks - 1, 0)
        further = pltpu.roll(residual, blocks - 2, 0)
        descent = jnp.dot(
            jnp.concatenate([further, ahead, residual], axis=1).astype(jnp.bfloat16),
            backward[atom],
            preferred_element_type=jnp.float32,
        )
        limit = limit_ref[atom]
        stepped = latent[rows_of(atom), :] + step_ref[atom] * descent
        latent[rows_of(atom), :] = allowed_ref[...] * (
            stepped - jnp.minimum(jnp.maximum(stepped, -limit), limit)
        )
        return carry

    def one_step(iteration, carry):
        lax.fori_loop(0, atoms, convolve, 0, unroll=8)
        lax.fori_loop(0, blocks, functools.partial(mix, matrix_ref=gram_ref), 0, unroll=4)
        lax.fori_loop(0, atoms, shrink, 0, unroll=8)
        return carry

    lax.fori_loop(0, steps, one_step, 0)
    for block in range(own):
        first = (HALO + block) * atoms
        latent_out[:, block * LANES : (block + 1) * LANES] = latent[first : first + atoms, :]
    if not last:
        return
    lax.fori_loop(0, atoms, convolve, 0, unroll=8)
    for block in range(own):
        first = (HALO + block) * atoms
        rebuilt_out[:, block * LANES : (block + 1) * LANES] = mixed[first : first + atoms, :]
    lax.fori_loop(HALO, HALO + own, functools.partial(mix, matrix_ref=plain_ref), 0, unroll=4)

    def lagged(atom, carry):
        codes = latent[rows_of(atom), :]
        codes = jnp.concatenate([pltpu.roll(codes, 2, 0), pltpu.roll(codes, 1, 0), codes], axis=1)
        codes = codes[HALO - 4 : HALO + own + 4]
        others = mixed[rows_of(atom), :][HALO - 4 : HALO + own + 4]
        place = lax.broadcasted_iota(jnp.int32, others.shape, 0)
        others = jnp.where((place >= 4) & (place < own + 4), others, 0.0)
        high = others.astype(jnp.bfloat16).astype(jnp.float32)
        pair = jnp.concatenate([high, others - high], axis=0).astype(jnp.bfloat16)
        twice = jnp.concatenate([codes, codes], axis=0).astype(jnp.bfloat16)
        total = lax.dot_general(
            pair, twice, (((0,), (0,)), ((), ())), preferred_element_type=jnp.float32
        )
        half = LANES // 2
        while half >= 1:
            total = total[:half] + pltpu.roll(total[half:], 3 * LANES - half, 1)
            half //= 2
        lags_out[pl.ds(atom, 1), :] = total
        return carry

    lax.fori_loop(0, atoms, lagged, 0, unroll=2)


def run_steps(steps, last, latent, projected, kernel_b, gram_matrix, step, limit, allowed, inside):
    atoms, width = latent.shape
    blocks = width // LANES
    own = blocks - 2 * HALO
    taps = kernel_b.astype(jnp.float32)
    tap_count = taps.shape[1]
    forward = jnp.pad(taps, ((0, 0), (0, 4 * LANES - tap_count)))
    backward = jnp.pad(taps[:, ::-1], ((0, 0), (1, 4 * LANES - tap_count - 1)))
    plain = gram_matrix - jnp.diag(jnp.diag(gram_matrix))
    out = [jax.ShapeDtypeStruct((atoms, own * LANES), jnp.float32)]
    if last:
        out.append(jax.ShapeDtypeStruct((atoms, own * LANES), jnp.float32))
        out.append(jax.ShapeDtypeStruct((atoms, 3 * LANES), jnp.float32))
    in_vmem = pl.BlockSpec(memory_space=pltpu.VMEM)
    in_smem = pl.BlockSpec(memory_space=pltpu.SMEM)
    return pl.pallas_call(
        functools.partial(steps_kernel, steps, last, atoms, blocks, own),
        out_shape=out,
        in_specs=[in_smem] * 2 + [in_vmem] * 8,
        out_specs=[in_vmem] * len(out),
        scratch_shapes=[pltpu.VMEM((blocks * atoms, LANES), jnp.float32)] * 3
        + [pltpu.VMEM((atoms, 3 * LANES, LANES), jnp.bfloat16)] * 2,
        compiler_params=pltpu.CompilerParams(vmem_limit_bytes=48 * 1024 * 1024),
        cost_estimate=pl.CostEstimate(
            flops=4 * steps * atoms * width * 3 * LANES, bytes_accessed=8 * atoms * width, transcendentals=0
        ),
    )(
        step, limit, latent, projected, forward, backward, split3(gram_matrix), split3(plain),
        allowed.reshape(blocks, LANES), inside.reshape(blocks, LANES),
    )


def widened(value):
    rim = HALO * LANES
    before = passed_along(value[:, value.shape[1] - rim :], "seg", 1)
    after = passed_along(value[:, :rim], "seg", -1)
    return jnp.concatenate([before, value, after], axis=1)


def whole_sum_kernel(axis, count, value_ref, out_ref, landed, send_sem, recv_sem):
    me = lax.axis_index(axis)
    barrier = pltpu.get_barrier_semaphore()
    for step in range(1, count):
        pl.semaphore_signal(
            barrier, inc=1, device_id={axis: lax.rem(me + step, count)},
            device_id_type=pl.DeviceIdType.MESH,
        )
    pl.semaphore_wait(barrier, count - 1)
    copies = []
    for step in range(1, count):
        copy = pltpu.make_async_remote_copy(
            src_ref=value_ref,
            dst_ref=landed.at[me],
            send_sem=send_sem.at[step],
            recv_sem=recv_sem.at[step],
            device_id={axis: lax.rem(me + step, count)},
            device_id_type=pl.DeviceIdType.MESH,
        )
        copy.start()
        copies.append(copy)
    landed[me] = value_ref[...]
    for copy in copies:
        copy.wait()
    total = landed[0]
    for slot in range(1, count):
        total = total + landed[slot]
    out_ref[...] = total


def shared_sum_kernel(axis, count, value_ref, out_ref, landed, part, spread, send_sem, recv_sem):
    me = lax.axis_index(axis)
    chunk = value_ref.shape[0] // count
    barrier = pltpu.get_barrier_semaphore()
    for step in range(1, count):
        pl.semaphore_signal(
            barrier, inc=1, device_id={axis: lax.rem(me + step, count)},
            device_id_type=pl.DeviceIdType.MESH,
        )
    pl.semaphore_wait(barrier, count - 1)
    copies = []
    for step in range(1, count):
        peer = lax.rem(me + step, count)
        copy = pltpu.make_async_remote_copy(
            src_ref=value_ref.at[pl.ds(pl.multiple_of(peer * chunk, 8), chunk)],
            dst_ref=landed.at[me],
            send_sem=send_sem.at[0, step],
            recv_sem=recv_sem.at[0, step],
            device_id={axis: peer},
            device_id_type=pl.DeviceIdType.MESH,
        )
        copy.start()
        copies.append(copy)
    landed[me] = value_ref[pl.ds(pl.multiple_of(me * chunk, 8), chunk), :]
    for copy in copies:
        copy.wait()
    total = landed[0]
    for slot in range(1, count):
        total = total + landed[slot]
    part[...] = total
    copies = []
    for step in range(1, count):
        peer = lax.rem(me + step, count)
        copy = pltpu.make_async_remote_copy(
            src_ref=part,
            dst_ref=spread.at[me],
            send_sem=send_sem.at[1, step],
            recv_sem=recv_sem.at[1, step],
            device_id={axis: peer},
            device_id_type=pl.DeviceIdType.MESH,
        )
        copy.start()
        copies.append(copy)
    spread[me] = part[...]
    for copy in copies:
        copy.wait()
    for slot in range(count):
        out_ref[slot * chunk : (slot + 1) * chunk, :] = spread[slot]


def device_sum(value, axis, shared, identity):
    count = lax.axis_size(axis)
    rows, columns = value.shape
    if shared:
        chunk = rows // count
        kernel = shared_sum_kernel
        scratch = [
            pltpu.VMEM((count, chunk, columns), jnp.float32),
            pltpu.VMEM((chunk, columns), jnp.float32),
            pltpu.VMEM((count, chunk, columns), jnp.float32),
            pltpu.SemaphoreType.DMA((2, count)),
            pltpu.SemaphoreType.DMA((2, count)),
        ]
    else:
        kernel = whole_sum_kernel
        scratch = [
            pltpu.VMEM((count, rows, columns), jnp.float32),
            pltpu.SemaphoreType.DMA((count,)),
            pltpu.SemaphoreType.DMA((count,)),
        ]
    return pl.pallas_call(
        functools.partial(kernel, axis, count),
        out_shape=jax.ShapeDtypeStruct((rows, columns), jnp.float32),
        in_specs=[pl.BlockSpec(memory_space=pltpu.VMEM)],
        out_specs=pl.BlockSpec(memory_space=pltpu.VMEM),
        scratch_shapes=scratch,
        compiler_params=pltpu.CompilerParams(
            collective_id=identity, has_side_effects=True, vmem_limit_bytes=24 * 1024 * 1024
        ),
        cost_estimate=pl.CostEstimate(
            flops=count * rows * columns, bytes_accessed=8 * count * rows * columns, transcendentals=0
        ),
    )(value)


def gram_sum(space):
    partial = jnp.dot(space.T, space, precision=highest)
    atoms = partial.shape[0]
    return device_sum(jnp.pad(partial, ((0, 0), (0, -atoms % LANES))), "chan", False, 1)[:, :atoms]


def projected_sum(space_b, signal):
    return device_sum(
        jnp.dot(space_b.T, signal, preferred_element_type=jnp.float32), "chan", True, 2
    )


def seg_sums(stats, cross, taps):
    rows, atoms = stats.shape
    small = jnp.concatenate([cross, taps], axis=1)
    small = jnp.pad(small, ((0, 0), (0, -small.shape[1] % LANES)))
    parts = small.shape[1] // LANES
    packed = [stats[: rows // 2], stats[rows // 2 :]]
    packed = [jnp.concatenate(packed, axis=1)] + [
        small[:, part * LANES : (part + 1) * LANES] for part in range(parts)
    ]
    packed = jnp.concatenate(packed, axis=0)
    total = packed.shape[0]
    packed = jnp.pad(packed, ((0, -total % (8 * lax.axis_size("seg"))), (0, 0)))
    summed = device_sum(packed, "seg", True, 3)
    halves = summed[: rows // 2]
    stats = jnp.concatenate([halves[:, :atoms], halves[:, atoms:]], axis=0)
    small = jnp.concatenate(
        [
            summed[rows // 2 + part * atoms : rows // 2 + (part + 1) * atoms]
            for part in range(parts)
        ],
        axis=1,
    )
    return stats, small[:, :atoms], small[:, atoms : atoms + taps.shape[1]]


def on_device(signal, spatial, temporal, start_codes, thresholds, step_sizes, breaks):
    chan_rows, seg_len = signal.shape
    atoms_all, tap_count = temporal.shape
    rim = HALO * LANES
    positions = lax.axis_index("seg") * seg_len - rim + lax.iota(jnp.int32, seg_len + 2 * rim)
    inside = (positions >= 0) & (positions < seg_len * lax.axis_size("seg"))
    crosses = (positions[None, :] < breaks[:, None]) & (
        breaks[:, None] < positions[None, :] + tap_count
    )
    allowed = jnp.where(jnp.any(crosses, axis=0) | ~inside, 0.0, 1.0).astype(jnp.float32)
    inside = inside.astype(jnp.float32)
    raw_start = gram_sum(spatial)
    scaling = 1.0 / jnp.sqrt(jnp.diag(raw_start) + epsilon)
    space_loc = spatial * scaling[None, :]
    gram_matrix = raw_start * scaling[:, None] * scaling[None, :]
    kernel = temporal / jnp.sqrt(jnp.sum(temporal * temporal, axis=1, keepdims=True) + epsilon)
    latent = start_codes
    limits = step_sizes * thresholds
    for sweep_index in range(OUTER):
        space_b = space_loc.astype(jnp.bfloat16)
        kernel_b = kernel.astype(jnp.bfloat16)
        projected = projected_sum(space_b, signal)
        wide = widened(projected)
        (latent,) = run_steps(
            ITERS // 2, False, widened(latent), wide, kernel_b, gram_matrix,
            step_sizes, limits, allowed, inside,
        )
        latent, rebuilt, lags = run_steps(
            ITERS - ITERS // 2, True, widened(latent), wide, kernel_b, gram_matrix,
            step_sizes, limits, allowed, inside,
        )
        taps_part = lags[:, 1 : tap_count + 1][:, ::-1]
        rebuilt_b = rebuilt.astype(jnp.bfloat16)
        stats, cross_gram, raw_kernel = seg_sums(
            jnp.dot(signal, rebuilt_b.T, preferred_element_type=jnp.float32),
            jnp.dot(rebuilt, rebuilt.T, precision=highest),
            taps_part,
        )
        raw_space = stats - jnp.dot(
            space_loc, cross_gram - jnp.diag(jnp.diag(cross_gram)), precision=highest
        )
        raw_gram = gram_sum(raw_space)
        scaling = 1.0 / jnp.sqrt(jnp.diag(raw_gram) + epsilon)
        space_loc = raw_space * scaling[None, :]
        gram_matrix = raw_gram * scaling[:, None] * scaling[None, :]
        kernel = raw_kernel / jnp.sqrt(
            jnp.sum(raw_kernel * raw_kernel, axis=1, keepdims=True) + epsilon
        )
    return (latent, space_loc, kernel)


def solution(mesh):
    placed = (P("chan", "seg"), P("chan", None), P(), P(None, "seg"), P(), P(), P())
    return jax.shard_map(
        on_device,
        mesh=mesh,
        in_specs=placed,
        out_specs=(P(None, "seg"), P("chan", None), P()),
        check_vma=False,
    )
```

```python
import functools
import jax
import jax.numpy as jnp
from jax import lax
from jax.experimental import pallas as pl
from jax.experimental.pallas import tpu as pltpu
from jax.sharding import PartitionSpec as P

ITERS = 10
OUTER = 2
LANES = 128
HALO = 12


epsilon = 1e-06
highest = lax.Precision.HIGHEST


def passed_along(value, axis, steps):
    count = lax.axis_size(axis)
    leading, last = (max(0, -steps), min(count, count - steps))
    return lax.ppermute(value, axis, [(source, source + steps) for source in range(leading, last)])


def split3(matrix):
    high = matrix.astype(jnp.bfloat16)
    low = (matrix - high.astype(jnp.float32)).astype(jnp.bfloat16)
    return jnp.concatenate([high, high, low], axis=1)


def steps_kernel(
    steps, last, atoms, blocks, own,
    step_ref, limit_ref, latent_in, proj_in, taps_ref, flipped_ref, gram_ref, plain_ref,
    allowed_ref, inside_ref,
    *rest,
):
    if last:
        latent_out, rebuilt_out, lags_out, latent, proj, mixed, forward, backward, stage = rest
    else:
        latent_out, latent, proj, mixed, forward, backward, _ = rest

    def spread(block, carry):
        rows = pl.ds(pl.multiple_of(block * atoms, atoms), atoms)
        columns = pl.ds(pl.multiple_of(block * LANES, LANES), LANES)
        latent[rows, :] = latent_in[:, columns]
        proj[rows, :] = proj_in[:, columns]
        return carry

    lax.fori_loop(0, blocks, spread, 0, unroll=4)

    def build(atom, carry):
        for source, target in ((taps_ref, forward), (flipped_ref, backward)):
            row = jnp.broadcast_to(source[pl.ds(atom, 1), :], (LANES, 4 * LANES))
            turned = pltpu.roll(row, 0, 1, stride=1, stride_axis=0).astype(jnp.bfloat16)
            for part in range(3):
                target[atom, part * LANES : (part + 1) * LANES, :] = turned[
                    :, part * LANES : (part + 1) * LANES
                ]
        return carry

    lax.fori_loop(0, atoms, build, 0, unroll=4)

    def rows_of(atom):
        return pl.ds(atom, blocks, stride=atoms)

    def window(values):
        return jnp.concatenate(
            [values, pltpu.roll(values, 1, 0), pltpu.roll(values, 2, 0)], axis=1
        ).astype(jnp.bfloat16)

    def convolve(atom, carry):
        mixed[rows_of(atom), :] = jnp.dot(
            window(latent[rows_of(atom), :]), forward[atom], preferred_element_type=jnp.float32
        )
        return carry

    def mix(pair, carry, matrix_ref):
        rows = pl.ds(pl.multiple_of(pair * 2 * atoms, 2 * atoms), 2 * atoms)
        both = mixed[rows, :]
        rebuilt = jnp.concatenate([both[:atoms], both[atoms:]], axis=1)
        high = rebuilt.astype(jnp.bfloat16)
        low = (rebuilt - high.astype(jnp.float32)).astype(jnp.bfloat16)
        blended = jnp.dot(
            matrix_ref[...],
            jnp.concatenate([high, low, high], axis=0),
            preferred_element_type=jnp.float32,
        )
        mixed[rows, :] = proj[rows, :] - jnp.concatenate(
            [blended[:, :LANES], blended[:, LANES:]], axis=0
        )
        return carry

    def shrink(atom, carry):
        residual = jnp.where(inside_ref[...] > 0.5, mixed[rows_of(atom), :], 0.0)
        ahead = pltpu.roll(residual, blocks - 1, 0)
        further = pltpu.roll(residual, blocks - 2, 0)
        descent = jnp.dot(
            jnp.concatenate([further, ahead, residual], axis=1).astype(jnp.bfloat16),
            backward[atom],
            preferred_element_type=jnp.float32,
        )
        limit = limit_ref[atom]
        stepped = latent[rows_of(atom), :] + step_ref[atom] * descent
        latent[rows_of(atom), :] = allowed_ref[...] * (
            stepped - jnp.minimum(jnp.maximum(stepped, -limit), limit)
        )
        return carry

    def one_step(iteration, carry):
        lax.fori_loop(0, atoms, convolve, 0, unroll=8)
        lax.fori_loop(0, blocks // 2, functools.partial(mix, matrix_ref=gram_ref), 0, unroll=4)
        lax.fori_loop(0, atoms, shrink, 0, unroll=8)
        return carry

    lax.fori_loop(0, steps, one_step, 0)
    for block in range(own):
        first = (HALO + block) * atoms
        latent_out[:, block * LANES : (block + 1) * LANES] = latent[first : first + atoms, :]
    if not last:
        return
    lax.fori_loop(0, atoms, convolve, 0, unroll=8)
    for block in range(own):
        first = (HALO + block) * atoms
        rebuilt_out[:, block * LANES : (block + 1) * LANES] = mixed[first : first + atoms, :]
    lax.fori_loop(
        HALO // 2, (HALO + own) // 2, functools.partial(mix, matrix_ref=plain_ref), 0, unroll=4
    )

    def lagged(atom, carry):
        codes = latent[rows_of(atom), :]
        codes = jnp.concatenate([pltpu.roll(codes, 2, 0), pltpu.roll(codes, 1, 0), codes], axis=1)
        codes = codes[HALO - 4 : HALO + own + 4]
        others = mixed[rows_of(atom), :][HALO - 4 : HALO + own + 4]
        place = lax.broadcasted_iota(jnp.int32, others.shape, 0)
        others = jnp.where((place >= 4) & (place < own + 4), others, 0.0)
        high = others.astype(jnp.bfloat16).astype(jnp.float32)
        pair = jnp.concatenate([high, others - high], axis=0).astype(jnp.bfloat16)
        twice = jnp.concatenate([codes, codes], axis=0).astype(jnp.bfloat16)
        total = lax.dot_general(
            pair, twice, (((0,), (0,)), ((), ())), preferred_element_type=jnp.float32
        )
        half = LANES // 2
        while half >= 8:
            total = total[:half] + pltpu.roll(total[half:], 3 * LANES - half, 1)
            half //= 2
        stage[atom] = total
        return carry

    lax.fori_loop(0, atoms, lagged, 0, unroll=8)
    total = stage[:, 0, :]
    for row in range(1, 8):
        total = total + pltpu.roll(stage[:, row, :], 3 * LANES - row, 1)
    lags_out[...] = total


def run_steps(steps, last, latent, projected, kernel_b, gram_matrix, step, limit, allowed, inside):
    atoms, width = latent.shape
    blocks = width // LANES
    own = blocks - 2 * HALO
    taps = kernel_b.astype(jnp.float32)
    tap_count = taps.shape[1]
    forward = jnp.pad(taps, ((0, 0), (0, 4 * LANES - tap_count)))
    backward = jnp.pad(taps[:, ::-1], ((0, 0), (1, 4 * LANES - tap_count - 1)))
    plain = gram_matrix - jnp.diag(jnp.diag(gram_matrix))
    out = [jax.ShapeDtypeStruct((atoms, own * LANES), jnp.float32)]
    if last:
        out.append(jax.ShapeDtypeStruct((atoms, own * LANES), jnp.float32))
        out.append(jax.ShapeDtypeStruct((atoms, 3 * LANES), jnp.float32))
    in_vmem = pl.BlockSpec(memory_space=pltpu.VMEM)
    in_smem = pl.BlockSpec(memory_space=pltpu.SMEM)
    return pl.pallas_call(
        functools.partial(steps_kernel, steps, last, atoms, blocks, own),
        out_shape=out,
        in_specs=[in_smem] * 2 + [in_vmem] * 8,
        out_specs=[in_vmem] * len(out),
        scratch_shapes=[pltpu.VMEM((blocks * atoms, LANES), jnp.float32)] * 3
        + [pltpu.VMEM((atoms, 3 * LANES, LANES), jnp.bfloat16)] * 2
        + [pltpu.VMEM((atoms, 8, 3 * LANES), jnp.float32)],
        compiler_params=pltpu.CompilerParams(vmem_limit_bytes=48 * 1024 * 1024),
        cost_estimate=pl.CostEstimate(
            flops=4 * steps * atoms * width * 3 * LANES, bytes_accessed=8 * atoms * width, transcendentals=0
        ),
    )(
        step, limit, latent, projected, forward, backward, split3(gram_matrix), split3(plain),
        allowed.reshape(blocks, LANES), inside.reshape(blocks, LANES),
    )


def widened(value):
    rim = HALO * LANES
    before = passed_along(value[:, value.shape[1] - rim :], "seg", 1)
    after = passed_along(value[:, :rim], "seg", -1)
    return jnp.concatenate([before, value, after], axis=1)


def whole_sum_kernel(axis, count, value_ref, out_ref, landed, send_sem, recv_sem):
    me = lax.axis_index(axis)
    barrier = pltpu.get_barrier_semaphore()
    for step in range(1, count):
        pl.semaphore_signal(
            barrier, inc=1, device_id={axis: lax.rem(me + step, count)},
            device_id_type=pl.DeviceIdType.MESH,
        )
    pl.semaphore_wait(barrier, count - 1)
    copies = []
    for step in range(1, count):
        copy = pltpu.make_async_remote_copy(
            src_ref=value_ref,
            dst_ref=landed.at[me],
            send_sem=send_sem.at[step],
            recv_sem=recv_sem.at[step],
            device_id={axis: lax.rem(me + step, count)},
            device_id_type=pl.DeviceIdType.MESH,
        )
        copy.start()
        copies.append(copy)
    landed[me] = value_ref[...]
    for copy in copies:
        copy.wait()
    total = landed[0]
    for slot in range(1, count):
        total = total + landed[slot]
    out_ref[...] = total


def shared_sum_kernel(axis, count, value_ref, out_ref, landed, part, spread, send_sem, recv_sem):
    me = lax.axis_index(axis)
    chunk = value_ref.shape[0] // count
    barrier = pltpu.get_barrier_semaphore()
    for step in range(1, count):
        pl.semaphore_signal(
            barrier, inc=1, device_id={axis: lax.rem(me + step, count)},
            device_id_type=pl.DeviceIdType.MESH,
        )
    pl.semaphore_wait(barrier, count - 1)
    copies = []
    for step in range(1, count):
        peer = lax.rem(me + step, count)
        copy = pltpu.make_async_remote_copy(
            src_ref=value_ref.at[pl.ds(pl.multiple_of(peer * chunk, 8), chunk)],
            dst_ref=landed.at[me],
            send_sem=send_sem.at[0, step],
            recv_sem=recv_sem.at[0, step],
            device_id={axis: peer},
            device_id_type=pl.DeviceIdType.MESH,
        )
        copy.start()
        copies.append(copy)
    landed[me] = value_ref[pl.ds(pl.multiple_of(me * chunk, 8), chunk), :]
    for copy in copies:
        copy.wait()
    total = landed[0]
    for slot in range(1, count):
        total = total + landed[slot]
    part[...] = total
    copies = []
    for step in range(1, count):
        peer = lax.rem(me + step, count)
        copy = pltpu.make_async_remote_copy(
            src_ref=part,
            dst_ref=spread.at[me],
            send_sem=send_sem.at[1, step],
            recv_sem=recv_sem.at[1, step],
            device_id={axis: peer},
            device_id_type=pl.DeviceIdType.MESH,
        )
        copy.start()
        copies.append(copy)
    spread[me] = part[...]
    for copy in copies:
        copy.wait()
    for slot in range(count):
        out_ref[slot * chunk : (slot + 1) * chunk, :] = spread[slot]


def device_sum(value, axis, shared, identity):
    count = lax.axis_size(axis)
    rows, columns = value.shape
    if shared:
        chunk = rows // count
        kernel = shared_sum_kernel
        scratch = [
            pltpu.VMEM((count, chunk, columns), jnp.float32),
            pltpu.VMEM((chunk, columns), jnp.float32),
            pltpu.VMEM((count, chunk, columns), jnp.float32),
            pltpu.SemaphoreType.DMA((2, count)),
            pltpu.SemaphoreType.DMA((2, count)),
        ]
    else:
        kernel = whole_sum_kernel
        scratch = [
            pltpu.VMEM((count, rows, columns), jnp.float32),
            pltpu.SemaphoreType.DMA((count,)),
            pltpu.SemaphoreType.DMA((count,)),
        ]
    return pl.pallas_call(
        functools.partial(kernel, axis, count),
        out_shape=jax.ShapeDtypeStruct((rows, columns), jnp.float32),
        in_specs=[pl.BlockSpec(memory_space=pltpu.VMEM)],
        out_specs=pl.BlockSpec(memory_space=pltpu.VMEM),
        scratch_shapes=scratch,
        compiler_params=pltpu.CompilerParams(
            collective_id=identity, has_side_effects=True, vmem_limit_bytes=24 * 1024 * 1024
        ),
        cost_estimate=pl.CostEstimate(
            flops=count * rows * columns, bytes_accessed=8 * count * rows * columns, transcendentals=0
        ),
    )(value)


def gram_sum(space):
    partial = jnp.dot(space.T, space, precision=highest)
    atoms = partial.shape[0]
    return device_sum(jnp.pad(partial, ((0, 0), (0, -atoms % LANES))), "chan", False, 1)[:, :atoms]


def projected_sum(space_b, signal):
    return device_sum(
        jnp.dot(space_b.T, signal, preferred_element_type=jnp.float32), "chan", True, 2
    )


def seg_sums(stats, cross, taps):
    rows, atoms = stats.shape
    small = jnp.concatenate([cross, taps], axis=1)
    small = jnp.pad(small, ((0, 0), (0, -small.shape[1] % LANES)))
    parts = small.shape[1] // LANES
    packed = [stats[: rows // 2], stats[rows // 2 :]]
    packed = [jnp.concatenate(packed, axis=1)] + [
        small[:, part * LANES : (part + 1) * LANES] for part in range(parts)
    ]
    packed = jnp.concatenate(packed, axis=0)
    total = packed.shape[0]
    packed = jnp.pad(packed, ((0, -total % (8 * lax.axis_size("seg"))), (0, 0)))
    summed = device_sum(packed, "seg", True, 3)
    halves = summed[: rows // 2]
    stats = jnp.concatenate([halves[:, :atoms], halves[:, atoms:]], axis=0)
    small = jnp.concatenate(
        [
            summed[rows // 2 + part * atoms : rows // 2 + (part + 1) * atoms]
            for part in range(parts)
        ],
        axis=1,
    )
    return stats, small[:, :atoms], small[:, atoms : atoms + taps.shape[1]]


def on_device(signal, spatial, temporal, start_codes, thresholds, step_sizes, breaks):
    chan_rows, seg_len = signal.shape
    atoms_all, tap_count = temporal.shape
    rim = HALO * LANES
    positions = lax.axis_index("seg") * seg_len - rim + lax.iota(jnp.int32, seg_len + 2 * rim)
    inside = (positions >= 0) & (positions < seg_len * lax.axis_size("seg"))
    crosses = (positions[None, :] < breaks[:, None]) & (
        breaks[:, None] < positions[None, :] + tap_count
    )
    allowed = jnp.where(jnp.any(crosses, axis=0) | ~inside, 0.0, 1.0).astype(jnp.float32)
    inside = inside.astype(jnp.float32)
    raw_start = gram_sum(spatial)
    scaling = 1.0 / jnp.sqrt(jnp.diag(raw_start) + epsilon)
    space_loc = spatial * scaling[None, :]
    gram_matrix = raw_start * scaling[:, None] * scaling[None, :]
    kernel = temporal / jnp.sqrt(jnp.sum(temporal * temporal, axis=1, keepdims=True) + epsilon)
    latent = start_codes
    limits = step_sizes * thresholds
    for sweep_index in range(OUTER):
        space_b = space_loc.astype(jnp.bfloat16)
        kernel_b = kernel.astype(jnp.bfloat16)
        projected = projected_sum(space_b, signal)
        wide = widened(projected)
        (latent,) = run_steps(
            ITERS // 2, False, widened(latent), wide, kernel_b, gram_matrix,
            step_sizes, limits, allowed, inside,
        )
        latent, rebuilt, lags = run_steps(
            ITERS - ITERS // 2, True, widened(latent), wide, kernel_b, gram_matrix,
            step_sizes, limits, allowed, inside,
        )
        taps_part = lags[:, 1 : tap_count + 1][:, ::-1]
        rebuilt_b = rebuilt.astype(jnp.bfloat16)
        stats, cross_gram, raw_kernel = seg_sums(
            jnp.dot(signal, rebuilt_b.T, preferred_element_type=jnp.float32),
            jnp.dot(rebuilt, rebuilt.T, precision=highest),
            taps_part,
        )
        raw_space = stats - jnp.dot(
            space_loc, cross_gram - jnp.diag(jnp.diag(cross_gram)), precision=highest
        )
        raw_gram = gram_sum(raw_space)
        scaling = 1.0 / jnp.sqrt(jnp.diag(raw_gram) + epsilon)
        space_loc = raw_space * scaling[None, :]
        gram_matrix = raw_gram * scaling[:, None] * scaling[None, :]
        kernel = raw_kernel / jnp.sqrt(
            jnp.sum(raw_kernel * raw_kernel, axis=1, keepdims=True) + epsilon
        )
    return (latent, space_loc, kernel)


def solution(mesh):
    placed = (P("chan", "seg"), P("chan", None), P(), P(None, "seg"), P(), P(), P())
    return jax.shard_map(
        on_device,
        mesh=mesh,
        in_specs=placed,
        out_specs=(P(None, "seg"), P("chan", None), P()),
        check_vma=False,
    )
```

```python
import functools
import jax
import jax.numpy as jnp
from jax import lax
from jax.experimental import pallas as pl
from jax.experimental.pallas import tpu as pltpu
from jax.sharding import PartitionSpec as P

ITERS = 10
OUTER = 2
LANES = 128
HALO = 12


epsilon = 1e-06
highest = lax.Precision.HIGHEST


def split3(matrix):
    high = matrix.astype(jnp.bfloat16)
    low = (matrix - high.astype(jnp.float32)).astype(jnp.bfloat16)
    return jnp.concatenate([high, high, low], axis=1)


def steps_kernel(
    steps, last, atoms, blocks, own,
    step_ref, limit_ref, latent_in, proj_in, taps_ref, flipped_ref, gram_ref, plain_ref,
    allowed_ref, inside_ref,
    *rest,
):
    if last:
        latent_out, rebuilt_out, lags_out, latent, proj, mixed, forward, backward, stage = rest
    else:
        latent_out, latent, proj, mixed, forward, backward, _ = rest

    def spread(block, carry):
        rows = pl.ds(pl.multiple_of(block * atoms, atoms), atoms)
        columns = pl.ds(pl.multiple_of(block * LANES, LANES), LANES)
        latent[rows, :] = latent_in[:, columns]
        proj[rows, :] = proj_in[:, columns]
        return carry

    lax.fori_loop(0, blocks, spread, 0, unroll=4)

    def build(atom, carry):
        for source, target in ((taps_ref, forward), (flipped_ref, backward)):
            row = jnp.broadcast_to(source[pl.ds(atom, 1), :], (LANES, 4 * LANES))
            turned = pltpu.roll(row, 0, 1, stride=1, stride_axis=0).astype(jnp.bfloat16)
            for part in range(3):
                target[atom, part * LANES : (part + 1) * LANES, :] = turned[
                    :, part * LANES : (part + 1) * LANES
                ]
        return carry

    lax.fori_loop(0, atoms, build, 0, unroll=4)

    def rows_of(atom):
        return pl.ds(atom, blocks, stride=atoms)

    def window(values):
        return jnp.concatenate(
            [values, pltpu.roll(values, 1, 0), pltpu.roll(values, 2, 0)], axis=1
        ).astype(jnp.bfloat16)

    def convolve(atom, carry):
        mixed[rows_of(atom), :] = jnp.dot(
            window(latent[rows_of(atom), :]), forward[atom], preferred_element_type=jnp.float32
        )
        return carry

    def mix(pair, carry, matrix_ref):
        rows = pl.ds(pl.multiple_of(pair * 2 * atoms, 2 * atoms), 2 * atoms)
        both = mixed[rows, :]
        rebuilt = jnp.concatenate([both[:atoms], both[atoms:]], axis=1)
        high = rebuilt.astype(jnp.bfloat16)
        low = (rebuilt - high.astype(jnp.float32)).astype(jnp.bfloat16)
        blended = jnp.dot(
            matrix_ref[...],
            jnp.concatenate([high, low, high], axis=0),
            preferred_element_type=jnp.float32,
        )
        mixed[rows, :] = proj[rows, :] - jnp.concatenate(
            [blended[:, :LANES], blended[:, LANES:]], axis=0
        )
        return carry

    def shrink(atom, carry):
        residual = jnp.where(inside_ref[...] > 0.5, mixed[rows_of(atom), :], 0.0)
        ahead = pltpu.roll(residual, blocks - 1, 0)
        further = pltpu.roll(residual, blocks - 2, 0)
        descent = jnp.dot(
            jnp.concatenate([further, ahead, residual], axis=1).astype(jnp.bfloat16),
            backward[atom],
            preferred_element_type=jnp.float32,
        )
        limit = limit_ref[atom]
        stepped = latent[rows_of(atom), :] + step_ref[atom] * descent
        latent[rows_of(atom), :] = allowed_ref[...] * (
            stepped - jnp.minimum(jnp.maximum(stepped, -limit), limit)
        )
        return carry

    def one_step(iteration, carry):
        lax.fori_loop(0, atoms, convolve, 0, unroll=8)
        lax.fori_loop(0, blocks // 2, functools.partial(mix, matrix_ref=gram_ref), 0, unroll=4)
        lax.fori_loop(0, atoms, shrink, 0, unroll=8)
        return carry

    lax.fori_loop(0, steps, one_step, 0)
    for block in range(own):
        first = (HALO + block) * atoms
        latent_out[:, block * LANES : (block + 1) * LANES] = latent[first : first + atoms, :]
    if not last:
        return
    lax.fori_loop(0, atoms, convolve, 0, unroll=8)
    for block in range(own):
        first = (HALO + block) * atoms
        rebuilt_out[:, block * LANES : (block + 1) * LANES] = mixed[first : first + atoms, :]
    lax.fori_loop(
        HALO // 2, (HALO + own) // 2, functools.partial(mix, matrix_ref=plain_ref), 0, unroll=4
    )

    def lagged(atom, carry):
        codes = latent[rows_of(atom), :]
        codes = jnp.concatenate([pltpu.roll(codes, 2, 0), pltpu.roll(codes, 1, 0), codes], axis=1)
        codes = codes[HALO - 4 : HALO + own + 4]
        others = mixed[rows_of(atom), :][HALO - 4 : HALO + own + 4]
        place = lax.broadcasted_iota(jnp.int32, others.shape, 0)
        others = jnp.where((place >= 4) & (place < own + 4), others, 0.0)
        high = others.astype(jnp.bfloat16).astype(jnp.float32)
        pair = jnp.concatenate([high, others - high], axis=0).astype(jnp.bfloat16)
        twice = jnp.concatenate([codes, codes], axis=0).astype(jnp.bfloat16)
        total = lax.dot_general(
            pair, twice, (((0,), (0,)), ((), ())), preferred_element_type=jnp.float32
        )
        half = LANES // 2
        while half >= 8:
            total = total[:half] + pltpu.roll(total[half:], 3 * LANES - half, 1)
            half //= 2
        stage[atom] = total
        return carry

    lax.fori_loop(0, atoms, lagged, 0, unroll=8)
    total = stage[:, 0, :]
    for row in range(1, 8):
        total = total + pltpu.roll(stage[:, row, :], 3 * LANES - row, 1)
    lags_out[...] = total


def run_steps(steps, last, latent, projected, kernel_b, gram_matrix, step, limit, allowed, inside):
    atoms, width = latent.shape
    blocks = width // LANES
    own = blocks - 2 * HALO
    taps = kernel_b.astype(jnp.float32)
    tap_count = taps.shape[1]
    forward = jnp.pad(taps, ((0, 0), (0, 4 * LANES - tap_count)))
    backward = jnp.pad(taps[:, ::-1], ((0, 0), (1, 4 * LANES - tap_count - 1)))
    plain = gram_matrix - jnp.diag(jnp.diag(gram_matrix))
    out = [jax.ShapeDtypeStruct((atoms, own * LANES), jnp.float32)]
    if last:
        out.append(jax.ShapeDtypeStruct((atoms, own * LANES), jnp.float32))
        out.append(jax.ShapeDtypeStruct((atoms, 3 * LANES), jnp.float32))
    in_vmem = pl.BlockSpec(memory_space=pltpu.VMEM)
    in_smem = pl.BlockSpec(memory_space=pltpu.SMEM)
    return pl.pallas_call(
        functools.partial(steps_kernel, steps, last, atoms, blocks, own),
        out_shape=out,
        in_specs=[in_smem] * 2 + [in_vmem] * 8,
        out_specs=[in_vmem] * len(out),
        scratch_shapes=[pltpu.VMEM((blocks * atoms, LANES), jnp.float32)] * 3
        + [pltpu.VMEM((atoms, 3 * LANES, LANES), jnp.bfloat16)] * 2
        + [pltpu.VMEM((atoms, 8, 3 * LANES), jnp.float32)],
        compiler_params=pltpu.CompilerParams(vmem_limit_bytes=48 * 1024 * 1024),
        cost_estimate=pl.CostEstimate(
            flops=4 * steps * atoms * width * 3 * LANES, bytes_accessed=8 * atoms * width, transcendentals=0
        ),
    )(
        step, limit, latent, projected, forward, backward, split3(gram_matrix), split3(plain),
        allowed.reshape(blocks, LANES), inside.reshape(blocks, LANES),
    )


def widen_kernel(count, arrays, *refs):
    values, outs = refs[:arrays], refs[arrays : 2 * arrays]
    landed, send_sem, recv_sem = refs[2 * arrays :]
    me = lax.axis_index("seg")
    rim = HALO * LANES
    own = values[0].shape[1]
    after, before = lax.rem(me + 1, count), lax.rem(me + count - 1, count)
    barrier = pltpu.get_barrier_semaphore()
    for peer in (after, before):
        pl.semaphore_signal(
            barrier, inc=1, device_id={"seg": peer}, device_id_type=pl.DeviceIdType.MESH
        )
    pl.semaphore_wait(barrier, 2)
    copies = []
    for index in range(arrays):
        for side, peer, first in ((0, after, own - rim), (1, before, 0)):
            copy = pltpu.make_async_remote_copy(
                src_ref=values[index].at[:, pl.ds(first, rim)],
                dst_ref=landed.at[index, side],
                send_sem=send_sem.at[index, side],
                recv_sem=recv_sem.at[index, side],
                device_id={"seg": peer},
                device_id_type=pl.DeviceIdType.MESH,
            )
            copy.start()
            copies.append(copy)
    for index in range(arrays):
        outs[index][:, rim : rim + own] = values[index][...]
    for copy in copies:
        copy.wait()
    for index in range(arrays):
        outs[index][:, :rim] = jnp.where(me > 0, landed[index, 0], 0.0)
        outs[index][:, rim + own :] = jnp.where(me < count - 1, landed[index, 1], 0.0)


def widened(*values):
    count = lax.axis_size("seg")
    arrays = len(values)
    rows, own = values[0].shape
    rim = HALO * LANES
    in_vmem = pl.BlockSpec(memory_space=pltpu.VMEM)
    return pl.pallas_call(
        functools.partial(widen_kernel, count, arrays),
        out_shape=[jax.ShapeDtypeStruct((rows, own + 2 * rim), jnp.float32)] * arrays,
        in_specs=[in_vmem] * arrays,
        out_specs=[in_vmem] * arrays,
        scratch_shapes=[
            pltpu.VMEM((arrays, 2, rows, rim), jnp.float32),
            pltpu.SemaphoreType.DMA((arrays, 2)),
            pltpu.SemaphoreType.DMA((arrays, 2)),
        ],
        compiler_params=pltpu.CompilerParams(
            collective_id=3 + arrays, has_side_effects=True, vmem_limit_bytes=24 * 1024 * 1024
        ),
        cost_estimate=pl.CostEstimate(
            flops=0, bytes_accessed=24 * arrays * rows * own, transcendentals=0
        ),
    )(*values)


def whole_sum_kernel(axis, count, value_ref, out_ref, landed, send_sem, recv_sem):
    me = lax.axis_index(axis)
    barrier = pltpu.get_barrier_semaphore()
    for step in range(1, count):
        pl.semaphore_signal(
            barrier, inc=1, device_id={axis: lax.rem(me + step, count)},
            device_id_type=pl.DeviceIdType.MESH,
        )
    pl.semaphore_wait(barrier, count - 1)
    copies = []
    for step in range(1, count):
        copy = pltpu.make_async_remote_copy(
            src_ref=value_ref,
            dst_ref=landed.at[me],
            send_sem=send_sem.at[step],
            recv_sem=recv_sem.at[step],
            device_id={axis: lax.rem(me + step, count)},
            device_id_type=pl.DeviceIdType.MESH,
        )
        copy.start()
        copies.append(copy)
    landed[me] = value_ref[...]
    for copy in copies:
        copy.wait()
    total = landed[0]
    for slot in range(1, count):
        total = total + landed[slot]
    out_ref[...] = total


def shared_sum_kernel(axis, count, value_ref, out_ref, landed, part, spread, send_sem, recv_sem):
    me = lax.axis_index(axis)
    chunk = value_ref.shape[0] // count
    barrier = pltpu.get_barrier_semaphore()
    for step in range(1, count):
        pl.semaphore_signal(
            barrier, inc=1, device_id={axis: lax.rem(me + step, count)},
            device_id_type=pl.DeviceIdType.MESH,
        )
    pl.semaphore_wait(barrier, count - 1)
    copies = []
    for step in range(1, count):
        peer = lax.rem(me + step, count)
        copy = pltpu.make_async_remote_copy(
            src_ref=value_ref.at[pl.ds(pl.multiple_of(peer * chunk, 8), chunk)],
            dst_ref=landed.at[me],
            send_sem=send_sem.at[0, step],
            recv_sem=recv_sem.at[0, step],
            device_id={axis: peer},
            device_id_type=pl.DeviceIdType.MESH,
        )
        copy.start()
        copies.append(copy)
    landed[me] = value_ref[pl.ds(pl.multiple_of(me * chunk, 8), chunk), :]
    for copy in copies:
        copy.wait()
    total = landed[0]
    for slot in range(1, count):
        total = total + landed[slot]
    part[...] = total
    copies = []
    for step in range(1, count):
        peer = lax.rem(me + step, count)
        copy = pltpu.make_async_remote_copy(
            src_ref=part,
            dst_ref=spread.at[me],
            send_sem=send_sem.at[1, step],
            recv_sem=recv_sem.at[1, step],
            device_id={axis: peer},
            device_id_type=pl.DeviceIdType.MESH,
        )
        copy.start()
        copies.append(copy)
    spread[me] = part[...]
    for copy in copies:
        copy.wait()
    for slot in range(count):
        out_ref[slot * chunk : (slot + 1) * chunk, :] = spread[slot]


def device_sum(value, axis, shared, identity):
    count = lax.axis_size(axis)
    rows, columns = value.shape
    if shared:
        chunk = rows // count
        kernel = shared_sum_kernel
        scratch = [
            pltpu.VMEM((count, chunk, columns), jnp.float32),
            pltpu.VMEM((chunk, columns), jnp.float32),
            pltpu.VMEM((count, chunk, columns), jnp.float32),
            pltpu.SemaphoreType.DMA((2, count)),
            pltpu.SemaphoreType.DMA((2, count)),
        ]
    else:
        kernel = whole_sum_kernel
        scratch = [
            pltpu.VMEM((count, rows, columns), jnp.float32),
            pltpu.SemaphoreType.DMA((count,)),
            pltpu.SemaphoreType.DMA((count,)),
        ]
    return pl.pallas_call(
        functools.partial(kernel, axis, count),
        out_shape=jax.ShapeDtypeStruct((rows, columns), jnp.float32),
        in_specs=[pl.BlockSpec(memory_space=pltpu.VMEM)],
        out_specs=pl.BlockSpec(memory_space=pltpu.VMEM),
        scratch_shapes=scratch,
        compiler_params=pltpu.CompilerParams(
            collective_id=identity, has_side_effects=True, vmem_limit_bytes=24 * 1024 * 1024
        ),
        cost_estimate=pl.CostEstimate(
            flops=count * rows * columns, bytes_accessed=8 * count * rows * columns, transcendentals=0
        ),
    )(value)


def gram_sum(space):
    partial = jnp.dot(space.T, space, precision=highest)
    atoms = partial.shape[0]
    return device_sum(jnp.pad(partial, ((0, 0), (0, -atoms % LANES))), "chan", False, 1)[:, :atoms]


def projected_sum(space_b, signal):
    return device_sum(
        jnp.dot(space_b.T, signal, preferred_element_type=jnp.float32), "chan", True, 2
    )


def seg_sums(stats, cross, taps):
    rows, atoms = stats.shape
    small = jnp.concatenate([cross, taps], axis=1)
    small = jnp.pad(small, ((0, 0), (0, -small.shape[1] % LANES)))
    parts = small.shape[1] // LANES
    packed = [stats[: rows // 2], stats[rows // 2 :]]
    packed = [jnp.concatenate(packed, axis=1)] + [
        small[:, part * LANES : (part + 1) * LANES] for part in range(parts)
    ]
    packed = jnp.concatenate(packed, axis=0)
    total = packed.shape[0]
    packed = jnp.pad(packed, ((0, -total % (8 * lax.axis_size("seg"))), (0, 0)))
    summed = device_sum(packed, "seg", True, 3)
    halves = summed[: rows // 2]
    stats = jnp.concatenate([halves[:, :atoms], halves[:, atoms:]], axis=0)
    small = jnp.concatenate(
        [
            summed[rows // 2 + part * atoms : rows // 2 + (part + 1) * atoms]
            for part in range(parts)
        ],
        axis=1,
    )
    return stats, small[:, :atoms], small[:, atoms : atoms + taps.shape[1]]


def on_device(signal, spatial, temporal, start_codes, thresholds, step_sizes, breaks):
    chan_rows, seg_len = signal.shape
    atoms_all, tap_count = temporal.shape
    rim = HALO * LANES
    positions = lax.axis_index("seg") * seg_len - rim + lax.iota(jnp.int32, seg_len + 2 * rim)
    inside = (positions >= 0) & (positions < seg_len * lax.axis_size("seg"))
    crosses = (positions[None, :] < breaks[:, None]) & (
        breaks[:, None] < positions[None, :] + tap_count
    )
    allowed = jnp.where(jnp.any(crosses, axis=0) | ~inside, 0.0, 1.0).astype(jnp.float32)
    inside = inside.astype(jnp.float32)
    raw_start = gram_sum(spatial)
    scaling = 1.0 / jnp.sqrt(jnp.diag(raw_start) + epsilon)
    space_loc = spatial * scaling[None, :]
    gram_matrix = raw_start * scaling[:, None] * scaling[None, :]
    kernel = temporal / jnp.sqrt(jnp.sum(temporal * temporal, axis=1, keepdims=True) + epsilon)
    latent = start_codes
    limits = step_sizes * thresholds
    for sweep_index in range(OUTER):
        space_b = space_loc.astype(jnp.bfloat16)
        kernel_b = kernel.astype(jnp.bfloat16)
        projected = projected_sum(space_b, signal)
        latent_wide, wide = widened(latent, projected)
        (latent,) = run_steps(
            ITERS // 2, False, latent_wide, wide, kernel_b, gram_matrix,
            step_sizes, limits, allowed, inside,
        )
        (latent_wide,) = widened(latent)
        latent, rebuilt, lags = run_steps(
            ITERS - ITERS // 2, True, latent_wide, wide, kernel_b, gram_matrix,
            step_sizes, limits, allowed, inside,
        )
        taps_part = lags[:, 1 : tap_count + 1][:, ::-1]
        rebuilt_b = rebuilt.astype(jnp.bfloat16)
        stats, cross_gram, raw_kernel = seg_sums(
            jnp.dot(signal, rebuilt_b.T, preferred_element_type=jnp.float32),
            jnp.dot(rebuilt, rebuilt.T, precision=highest),
            taps_part,
        )
        raw_space = stats - jnp.dot(
            space_loc, cross_gram - jnp.diag(jnp.diag(cross_gram)), precision=highest
        )
        raw_gram = gram_sum(raw_space)
        scaling = 1.0 / jnp.sqrt(jnp.diag(raw_gram) + epsilon)
        space_loc = raw_space * scaling[None, :]
        gram_matrix = raw_gram * scaling[:, None] * scaling[None, :]
        kernel = raw_kernel / jnp.sqrt(
            jnp.sum(raw_kernel * raw_kernel, axis=1, keepdims=True) + epsilon
        )
    return (latent, space_loc, kernel)


def solution(mesh):
    placed = (P("chan", "seg"), P("chan", None), P(), P(None, "seg"), P(), P(), P())
    return jax.shard_map(
        on_device,
        mesh=mesh,
        in_specs=placed,
        out_specs=(P(None, "seg"), P("chan", None), P()),
        check_vma=False,
    )
```
